256 devices in a mesh: fsdp: 32 (over x, z_hi, y), tensor: 8 (over z_lo, core).
Axes of the slice: x: 4, y: 4, z: 8 (z_hi: 2, z_lo: 4; z = z_hi * 4 + z_lo), core: 2. Of those that a mesh axis runs over, the one named last changes fastest.
Arguments:
- coeffs: bfloat16 [32768, 512], P('fsdp'), may hold values from -6 to 6
- pca_basis: bfloat16 [8192, 512], P('fsdp'), may hold values from -0.25 to 0.25
- w_gate: bfloat16 [8192, 14336], P('fsdp', 'tensor'), may hold values from -0.0625 to 0.0625
- w_up: bfloat16 [8192, 14336], P('fsdp', 'tensor'), may hold values from -0.0625 to 0.0625
- grad_hidden: bfloat16 [32768, 14336], P('fsdp', 'tensor'), may hold values from -1.1953125 to 1.1953125
Outputs:
- grad_coeffs: bfloat16 [32768, 512], P(('fsdp', 'tensor'))
- gate_grad_core: float32 [512, 14336], P('fsdp', 'tensor')
- up_grad_core: float32 [512, 14336], P('fsdp', 'tensor')
The draws below stay inside these ranges and needn't reach their ends.
All inputs are finite; a program needn't handle non-finite values.
Results may differ from the reference program's by a relative error of at most 0.03.
Values may be sent and summed in bfloat16 or wider, within the bound.
No kernel may reach another device: no remote copies, remote signals or barrier semaphores. Data moves between devices by JAX's collectives and lax.ppermute only.
A program may use at most 64 MiB of HBM per device.

```python
import math
import jax
import jax.numpy as jnp
from jax import lax

D = 8192
FF = 14336
R = 512
TOK_DEV = 1024
TOKENS = 32768
N_FSDP = 32


def block_levels(key, dims, pieces, least, top_value):
    def one(axis_at, parts):
        steps = jax.random.uniform(jax.random.fold_in(jax.random.fold_in(key, 6), axis_at), (parts,), jnp.float32, least / len(pieces), top_value / len(pieces))
        return jnp.repeat(jnp.exp(steps), dims[axis_at] // parts).reshape((-1,) + (1,) * (len(dims) - axis_at - 1))

    level = one(*pieces[0])
    for cut in pieces[1:]:
        level = level * one(*cut)
    return level


def gaussian(own_key, shape, width, bound, pieces=(), kind=jnp.bfloat16):
    entries = width * jax.random.normal(own_key, shape, jnp.float32)
    if pieces:
        entries = entries * block_levels(own_key, shape, pieces, -0.22, 0.18)
    return jnp.clip(entries, -bound, bound).astype(kind)


def setup_inputs(seed: int = 0) -> dict:
    splits = jax.random.split(jax.random.key(seed), 6)
    return {
        "coeffs": gaussian(splits[0], (TOKENS, R), 1.0, 6.0, ((0, 32),)),
        "pca_basis": gaussian(splits[1], (D, R), R ** -0.5, 0.25, ((0, 32),)),
        "w_gate": gaussian(splits[2], (D, FF), D ** -0.5, 0.0625, ((0, 32), (1, 8))),
        "w_up": gaussian(splits[3], (D, FF), D ** -0.5, 0.0625, ((0, 32), (1, 8))),
        "grad_hidden": gaussian(splits[4], (TOKENS, FF), 0.2, 1.1953125, ((0, 32), (1, 8))),
    }


def reference(coeffs, pca_basis, w_gate, w_up, grad_hidden):
    gate_core = jnp.dot(pca_basis.T, w_gate, preferred_element_type=jnp.float32).astype(jnp.bfloat16)
    up_core = jnp.dot(pca_basis.T, w_up, preferred_element_type=jnp.float32).astype(jnp.bfloat16)
    token_scale = 1.0 / math.sqrt(TOKENS)

    def one_block(totals, block_index):
        first_row = (block_index * TOK_DEV).astype(jnp.int32)
        row_block = lax.dynamic_slice_in_dim(coeffs, first_row, TOK_DEV, 0)
        grad_block = lax.dynamic_slice_in_dim(grad_hidden, first_row, TOK_DEV, 0)
        gate = jnp.dot(row_block, gate_core, preferred_element_type=jnp.float32)
        upward = jnp.dot(row_block, up_core, preferred_element_type=jnp.float32)
        sigmoid_gate = jax.nn.sigmoid(gate)
        grad_block = grad_block.astype(jnp.float32)
        grad_gate = (grad_block * upward * sigmoid_gate * (1.0 + gate * (1.0 - sigmoid_gate))).astype(jnp.bfloat16)
        grad_up = (grad_block * (gate * sigmoid_gate)).astype(jnp.bfloat16)
        coeff_block = jnp.dot(grad_gate, gate_core.T, preferred_element_type=jnp.float32)
        coeff_block = coeff_block + jnp.dot(grad_up, up_core.T, preferred_element_type=jnp.float32)
        gate_total = totals[0] + jnp.dot(row_block.T, grad_gate, preferred_element_type=jnp.float32)
        up_total = totals[1] + jnp.dot(row_block.T, grad_up, preferred_element_type=jnp.float32)
        return ((gate_total, up_total), coeff_block.astype(jnp.bfloat16))
    zeros_core = jnp.zeros((R, FF), jnp.float32)
    totals, coeff_blocks = lax.scan(one_block, (zeros_core, zeros_core), jnp.arange(N_FSDP, dtype=jnp.int32))
    grad_coeffs = coeff_blocks.reshape(TOKENS, R)
    return (grad_coeffs, totals[0] * token_scale, totals[1] * token_scale)
```

```python
import functools
import math

import jax
import jax.numpy as jnp
from jax import lax
from jax.experimental import pallas as pl
from jax.experimental.pallas import tpu as pltpu
from jax.sharding import PartitionSpec as P

BF16, F32 = jnp.bfloat16, jnp.float32
BOTH = ("fsdp", "tensor")
CHUNKS = 2
MIB = 1 << 20
SMEM = pl.BlockSpec(memory_space=pltpu.SMEM)
VMEM = pl.BlockSpec(memory_space=pltpu.VMEM)


def shift(ring, k):
    pairs = []
    for x in range(4):
        for z in range(2):
            for y in range(4):
                for t in range(8):
                    along_y = (t % 2 == 0) == (ring == "a")
                    u, v = (x, (y + k) % 4) if along_y else ((x + k) % 4, y)
                    pairs.append(((x * 8 + z * 4 + y) * 8 + t, (u * 8 + z * 4 + v) * 8 + t))
    return pairs


SHIFTS = {(ring, k): shift(ring, k) for ring in "ab" for k in (1, 2, 3)}
SWAP_Z = [(f * 8 + t, (f ^ 4) * 8 + t) for f in range(32) for t in range(8)]


def send(pieces, ring):
    return [lax.ppermute(piece, BOTH, SHIFTS[ring, k + 1]) for k, piece in enumerate(pieces)]


def call(body, out_shape, n_in, flops=0, moved=0, scratch=(), limit=16, name=None):
    outs = jax.tree.map(lambda _: VMEM, out_shape)
    return pl.pallas_call(
        body,
        out_shape=out_shape,
        in_specs=[SMEM] + [VMEM] * n_in,
        out_specs=outs,
        scratch_shapes=list(scratch),
        compiler_params=pltpu.CompilerParams(vmem_limit_bytes=limit * MIB),
        cost_estimate=pl.CostEstimate(flops=flops, bytes_accessed=moved, transcendentals=0),
        name=name,
    )


def spread(own, sent, rows, mine, size):
    for k in range(4):
        block = lax.rem(mine + k, 4)
        for which in range(2):
            value = rows(which, pl.multiple_of(block * size, size), size)
            ref = own if k == 0 else sent[k - 1]
            ref[which] = value.astype(ref.dtype)


def cores_body(place, basis, w_gate, w_up, own, p1, p2, p3, total):
    contract = (((0,), (0,)), ((), ()))
    total[0] = lax.dot_general(basis[...], w_gate[...], contract, preferred_element_type=F32)
    total[1] = lax.dot_general(basis[...], w_up[...], contract, preferred_element_type=F32)
    spread(own, (p1, p2, p3), lambda w, first, n: total[w, pl.ds(first, n), :], place[0], 128)


def partial_cores(place, basis, w_gate, w_up, chunk, cols):
    piece = jax.ShapeDtypeStruct((2, 128, cols), BF16)
    depth = basis.shape[0]
    block = pl.BlockSpec((depth, cols), lambda i: (0, chunk))
    return pl.pallas_call(
        cores_body,
        grid=(1,),
        out_shape=[jax.ShapeDtypeStruct((2, 128, cols), F32), piece, piece, piece],
        in_specs=[SMEM, VMEM, block, block],
        out_specs=[VMEM] * 4,
        scratch_shapes=[pltpu.VMEM((2, 512, cols), F32)],
        compiler_params=pltpu.CompilerParams(vmem_limit_bytes=16 * MIB),
        cost_estimate=pl.CostEstimate(
            flops=4 * depth * 512 * cols, bytes_accessed=4 * MIB, transcendentals=0
        ),
        name="partial_cores",
    )(place, basis, w_gate, w_up)


def relay_body(place, own, r1, r2, r3, kept, p1, p2, p3, *, slot, size):
    def rows(which, first, n):
        at = (which, pl.ds(first, n), slice(None))
        return own[at] + r1[at].astype(F32) + r2[at].astype(F32) + r3[at].astype(F32)

    spread(kept, (p1, p2, p3), rows, place[slot], size)


def relay(place, own, got, cols):
    piece = jax.ShapeDtypeStruct((2, 32, cols), BF16)
    return call(
        functools.partial(relay_body, slot=1, size=32),
        [jax.ShapeDtypeStruct((2, 32, cols), F32), piece, piece, piece],
        4,
        moved=MIB,
        name="relay",
    )(place, own, *got)


def sum4_body(place, own, r1, r2, r3, out):
    out[...] = (
        own[...] + r1[...].astype(F32) + r2[...].astype(F32) + r3[...].astype(F32)
    ).astype(out.dtype)


def add2_body(place, a, b, out):
    out[...] = (a[...].astype(F32) + b[...].astype(F32)).astype(out.dtype)


def join_body(place, own, r1, r2, r3, out, *, slot, size):
    for k, ref in enumerate((own, r1, r2, r3)):
        first = pl.multiple_of(lax.rem(place[slot] + 4 - k, 4) * size, size)
        out[:, pl.ds(first, size), :] = ref[...]


def reduce_cores(place, own, pieces, cols):
    kept, *pieces = relay(place, own, send(pieces, "a"), cols)
    piece = jax.ShapeDtypeStruct((2, 32, cols), BF16)
    half = call(sum4_body, piece, 4, moved=MIB, name="sum4")(place, kept, *send(pieces, "b"))
    core = call(add2_body, piece, 2, moved=MIB, name="add2")(
        place, half, lax.ppermute(half, BOTH, SWAP_Z)
    )
    got = send([core] * 3, "b")
    block = call(
        functools.partial(join_body, slot=1, size=32),
        jax.ShapeDtypeStruct((2, 128, cols), BF16),
        4,
        moved=MIB,
        name="join",
    )(place, core, *got)
    return [block] + send([block] * 3, "a")


def main_body(scale, first, place, coeffs, c0, c1, c2, c3, hidden, *rest):
    if first:
        dcoeffs, own, p1, p2, p3, core, grads = rest
    else:
        before, dcoeffs, own, p1, p2, p3, core, grads = rest
    step, steps = pl.program_id(0), pl.num_programs(0)

    @pl.when(step == 0)
    def _():
        join_body(place, c0, c1, c2, c3, core, slot=0, size=128)

    x = coeffs[...]
    gate = jnp.dot(x, core[0], preferred_element_type=F32)
    upward = jnp.dot(x, core[1], preferred_element_type=F32)
    sig = 0.5 * jnp.tanh(0.5 * gate) + 0.5
    scaled = hidden[...].astype(F32) * sig
    grad_gate = (scaled * upward * (1.0 + gate * (1.0 - sig))).astype(BF16)
    grad_up = (scaled * gate).astype(BF16)
    contract = (((1,), (1,)), ((), ()))
    total = lax.dot_general(grad_gate, core[0], contract, preferred_element_type=F32)
    total += lax.dot_general(grad_up, core[1], contract, preferred_element_type=F32)
    if not first:
        total += before[...]
    dcoeffs[...] = total.astype(dcoeffs.dtype)
    contract = (((0,), (0,)), ((), ()))
    gate_term = lax.dot_general(x, grad_gate, contract, preferred_element_type=F32)
    up_term = lax.dot_general(x, grad_up, contract, preferred_element_type=F32)

    @pl.when(step == 0)
    def _():
        grads[0], grads[1] = gate_term, up_term

    @pl.when(step > 0)
    def _():
        grads[0] += gate_term
        grads[1] += up_term

    @pl.when(step == steps - 1)
    def _():
        for k, ref in enumerate((own, p1, p2, p3)):
            block = lax.rem(place[0] + k, 4)
            for s in range(8):
                row = block * place[2] + (s // 2) * place[3] + (s % 2) * 64
                for which in range(2):
                    value = grads[which, pl.ds(pl.multiple_of(row, 16), 16), :] * scale
                    ref[which, s * 16 : s * 16 + 16, :] = value.astype(ref.dtype)


def main(place, coeffs, cores, hidden, before, chunk, cols, scale):
    tokens, rank = coeffs.shape
    tile = 256
    first = before is None
    piece = jax.ShapeDtypeStruct((2, 128, cols), BF16)
    whole = pl.BlockSpec((2, 128, cols), lambda i: (0, 0, 0))
    row_block = pl.BlockSpec((tile, rank), lambda i: (i, 0))
    return pl.pallas_call(
        functools.partial(main_body, scale, first),
        grid=(tokens // tile,),
        out_shape=[
            jax.ShapeDtypeStruct((tokens, rank), F32 if first else BF16),
            jax.ShapeDtypeStruct((2, 128, cols), F32),
            piece,
            piece,
            piece,
        ],
        in_specs=[SMEM, row_block]
        + [whole] * 4
        + [pl.BlockSpec((tile, cols), lambda i: (i, chunk))]
        + ([] if first else [row_block]),
        out_specs=[row_block] + [whole] * 4,
        scratch_shapes=[pltpu.VMEM((2, rank, cols), BF16), pltpu.VMEM((2, rank, cols), F32)],
        compiler_params=pltpu.CompilerParams(vmem_limit_bytes=40 * MIB),
        cost_estimate=pl.CostEstimate(
            flops=12 * tokens * rank * cols,
            bytes_accessed=10 * MIB,
            transcendentals=tokens * cols,
        ),
        name="main",
    )(place, coeffs, *cores, hidden, *([] if first else [before]))


def halve_body(place, own, r1, r2, r3, kept, sent):
    for z in range(2):
        rows = slice(16 * z, 16 * z + 16)
        value = (
            own[:, rows] + r1[:, rows].astype(F32) + r2[:, rows].astype(F32) + r3[:, rows].astype(F32)
        )

        @pl.when(place[4] == z)
        def _():
            kept[...] = value

        @pl.when(place[4] != z)
        def _():
            sent[...] = value.astype(BF16)


def last_body(place, kept0, got0, kept1, got1, gate, up):
    cols = kept0.shape[2]
    for which, out in enumerate((gate, up)):
        out[:, :cols] = kept0[which] + got0[which].astype(F32)
        out[:, cols:] = kept1[which] + got1[which].astype(F32)


def scatter_grads(place, own, pieces, cols):
    kept, *pieces = relay(place, own, send(pieces, "a"), cols)
    kept, sent = call(
        halve_body,
        [jax.ShapeDtypeStruct((2, 16, cols), F32), jax.ShapeDtypeStruct((2, 16, cols), BF16)],
        4,
        moved=MIB,
        name="halve",
    )(place, kept, *send(pieces, "b"))
    return kept, lax.ppermute(sent, BOTH, SWAP_Z)


def local(coeffs, pca_basis, w_gate, w_up, grad_hidden):
    fsdp, core = lax.axis_index("fsdp"), lax.axis_index("tensor") % 2
    x, z, y = fsdp // 8, fsdp // 4 % 2, fsdp % 4
    a, b = jnp.where(core == 0, y, x), jnp.where(core == 0, x, y)
    stride_a, stride_b = jnp.where(core == 0, 16, 128), jnp.where(core == 0, 128, 16)
    place = jnp.stack([a, b, stride_a, stride_b, z]).astype(jnp.int32)
    width = w_gate.shape[1]
    cols = width // CHUNKS
    scale = 1.0 / math.sqrt(coeffs.shape[0] * 32)

    parts = [partial_cores(place, pca_basis, w_gate, w_up, c, cols) for c in range(CHUNKS)]
    cores = [reduce_cores(place, own, pieces, cols) for own, *pieces in parts]
    total, ends = None, []
    for c in range(CHUNKS):
        total, own, *pieces = main(place, coeffs, cores[c], grad_hidden, total, c, cols, scale)
        ends += scatter_grads(place, own, pieces, cols)
    grad_coeffs = lax.psum_scatter(total, "tensor", scatter_dimension=0, tiled=True)
    out = jax.ShapeDtypeStruct((16, width), F32)
    gate_grad, up_grad = call(last_body, [out, out], 4, moved=MIB, name="last")(place, *ends)
    return grad_coeffs, gate_grad, up_grad


def solution(mesh):
    placed = (
        P("fsdp", None),
        P("fsdp", None),
        P("fsdp", "tensor"),
        P("fsdp", "tensor"),
        P("fsdp", "tensor"),
    )
    return jax.shard_map(
        local,
        mesh=mesh,
        in_specs=placed,
        out_specs=(P(BOTH, None), P("fsdp", "tensor"), P("fsdp", "tensor")),
        check_vma=False,
    )
```

```python
import functools
import math

import jax
import jax.numpy as jnp
from jax import lax
from jax.experimental import pallas as pl
from jax.experimental.pallas import tpu as pltpu
from jax.sharding import PartitionSpec as P

BF16, F32 = jnp.bfloat16, jnp.float32
BOTH = ("fsdp", "tensor")
WIDTHS = (896, 896)
MIB = 1 << 20
SLICES = 4
K1_LIMIT = 58
SMEM = pl.BlockSpec(memory_space=pltpu.SMEM)
VMEM = pl.BlockSpec(memory_space=pltpu.VMEM)
ANY = pl.BlockSpec(memory_space=pl.ANY)
HBM = pl.BlockSpec(memory_space=pltpu.HBM)
PLACES = [(x, z, y, t) for x in range(4) for z in range(2) for y in range(4) for t in range(8)]


def index(x, z, y, t):
    return (x * 8 + z * 4 + y) * 8 + t


def along_y(t, ring):
    return (t % 2 == 0) == (ring == "a")


def shift(ring, k):
    pairs = []
    for x, z, y, t in PLACES:
        u, v = (x, (y + k) % 4) if along_y(t, ring) else ((x + k) % 4, y)
        pairs.append((index(x, z, y, t), index(u, z, v, t)))
    return pairs


SHIFTS = {ring: [shift(ring, k) for k in (1, 2, 3)] for ring in "ab"}
SWAP_Z = [(index(x, z, y, t), index(x, 1 - z, y, t)) for x, z, y, t in PLACES]
SWAP_CORE = [(t, t ^ 1) for t in range(8)]
SWAP_LOW = [[(t, t ^ 2 * bit) for t in range(8)] for bit in (1, 2)]


def send(pieces, ring):
    return [lax.ppermute(piece, BOTH, SHIFTS[ring][k]) for k, piece in enumerate(pieces)]


def swap_z(piece):
    return lax.ppermute(piece, BOTH, SWAP_Z)


def like(*shape, kind=BF16):
    return jax.ShapeDtypeStruct(shape, kind)


def call(body, out_shape, ins, after=(), limit=16, moved=MIB, name=None):
    n, skip = len(ins), len(after)

    def kernel(*refs):
        body(*refs[:n], *refs[n + skip :])

    return pl.pallas_call(
        kernel,
        out_shape=out_shape,
        in_specs=[SMEM] + [VMEM] * (n - 1) + [ANY] * skip,
        out_specs=jax.tree.map(lambda _: VMEM, out_shape),
        compiler_params=pltpu.CompilerParams(vmem_limit_bytes=limit * MIB),
        cost_estimate=pl.CostEstimate(flops=0, bytes_accessed=moved, transcendentals=0),
        name=name,
    )(*ins, *after)


def cores_body(place, basis_hbm, gate_hbm, up_hbm, own, p1, p2, p3, basis, weights, sems):
    depth = basis.shape[0]
    rows = depth // SLICES
    copies = [pltpu.make_async_copy(basis_hbm, basis, sems.at[2 * SLICES])]
    for which, source in enumerate((gate_hbm, up_hbm)):
        for i in range(SLICES):
            at = pl.ds(i * rows, rows)
            sem = sems.at[which * SLICES + i]
            copies.append(pltpu.make_async_copy(source.at[at, :], weights.at[which, at, :], sem))
    for copy in copies:
        copy.start()
    copies[0].wait()
    contract = (((0,), (0,)), ((), ()))
    for which in range(2):
        for copy in copies[1 + which * SLICES : 1 + which * SLICES + SLICES]:
            copy.wait()
        for k, ref in ((2, p2), (1, p1), (3, p3), (0, own)):
            block = lax.rem(place[0] + k, 4)
            part = basis[:, pl.ds(pl.multiple_of(block * 128, 128), 128)]
            total = lax.dot_general(part, weights[which], contract, preferred_element_type=F32)
            ref[which] = total.astype(ref.dtype)


def partial_cores(place, basis, w_gate, w_up):
    depth, width = w_gate.shape
    return pl.pallas_call(
        cores_body,
        out_shape=[like(2, 128, width)] * 4,
        in_specs=[SMEM, HBM, HBM, HBM],
        out_specs=[VMEM] * 4,
        scratch_shapes=[
            pltpu.VMEM(basis.shape, BF16),
            pltpu.VMEM((2, depth, width), BF16),
            pltpu.SemaphoreType.DMA((2 * SLICES + 1,)),
        ],
        compiler_params=pltpu.CompilerParams(vmem_limit_bytes=K1_LIMIT * MIB),
        cost_estimate=pl.CostEstimate(
            flops=4 * depth * basis.shape[1] * width, bytes_accessed=6 * MIB, transcendentals=0
        ),
        name="partial_cores",
    )(place, basis, w_gate, w_up)


def add4(own, r1, r2, r3, at):
    return (own[at].astype(F32) + r1[at].astype(F32)) + (r2[at].astype(F32) + r3[at].astype(F32))


def relay_body(place, own, r1, r2, r3, *outs):
    for k in range(4):
        rows = pl.ds(pl.multiple_of(lax.rem(place[1] + k, 4) * 32, 32), 32)
        first = 0
        for ref in outs[k::4]:
            at = (slice(None), rows, slice(first, first + ref.shape[2]))
            ref[...] = add4(own, r1, r2, r3, at).astype(ref.dtype)
            first += ref.shape[2]


def relay(place, own, pieces, widths, after=()):
    outs = []
    for cols in widths:
        outs += [like(2, 32, cols, kind=F32)] + [like(2, 32, cols)] * 3
    outs = call(relay_body, outs, (place, own, *send(pieces, "a")), after, name="relay")
    return [outs[4 * c : 4 * c + 4] for c in range(len(widths))]


def regroup_body(place, c0, c1, c2, c3, own, r1, r2, r3, *outs):
    first = c0.shape[2]
    for k, (before, ref) in enumerate(zip((c0, c1, c2, c3), outs)):
        rows = pl.ds(pl.multiple_of(lax.rem(place[1] + k, 4) * 32, 32), 32)
        value = add4(own, r1, r2, r3, (slice(None), rows, slice(None)))
        ref[:, :, :first] = before[...]
        ref[:, :, first:] = value.astype(ref.dtype)


def sum4_body(place, own, r1, r2, r3, out):
    out[...] = add4(own, r1, r2, r3, ...).astype(out.dtype)


def add2_body(place, a, b, out):
    out[...] = (a[...].astype(F32) + b[...].astype(F32)).astype(BF16)


def join_body(place, *refs):
    outs = refs[len(refs) // 5 * 4 :]
    for chunk, out in enumerate(outs):
        for k, ref in enumerate(refs[4 * chunk : 4 * chunk + 4]):
            at = pl.ds(pl.multiple_of(lax.rem(place[1] + 4 - k, 4) * 32, 32), 32)
            out[:, at, :] = ref[...]


def main_body(scale, start, place, coeffs, c0, c1, c2, c3, hidden_hbm, *rest):
    first = start == 0
    if first:
        dcoeffs, own, p1, p2, p3, core, grads, hidden, sems = rest
    else:
        before, kept, sent, own, p1, p2, p3, core, grads, hidden, sems = rest
    step, steps = pl.program_id(0), pl.num_programs(0)
    tile = coeffs.shape[0]

    def fetch(i):
        rows = pl.ds(pl.multiple_of(i * tile, tile), tile)
        source = hidden_hbm.at[rows, pl.ds(start, hidden.shape[2])]
        return pltpu.make_async_copy(source, hidden.at[i], sems.at[i])

    @pl.when(step == 0)
    def _():
        for i in range(hidden.shape[0]):
            fetch(i).start()
        for k, ref in enumerate((c0, c1, c2, c3)):
            at = pl.multiple_of(lax.rem(place[0] + 4 - k, 4) * 128, 128)
            core[:, pl.ds(at, 128), :] = ref[...]

    x = coeffs[...]
    gate = jnp.dot(x, core[0], preferred_element_type=F32)
    upward = jnp.dot(x, core[1], preferred_element_type=F32)
    sig = 0.5 * jnp.tanh(0.5 * gate) + 0.5
    fetch(step).wait()
    scaled = hidden[step].astype(F32) * sig
    grad_gate = (scaled * upward * (1.0 + gate * (1.0 - sig))).astype(BF16)
    grad_up = (scaled * gate).astype(BF16)
    contract = (((1,), (1,)), ((), ()))
    total = lax.dot_general(grad_gate, core[0], contract, preferred_element_type=F32)
    total += lax.dot_general(grad_up, core[1], contract, preferred_element_type=F32)
    if first:
        dcoeffs[...] = total
    else:
        total += before[...]
        for half in range(2):
            rows = total[128 * half : 128 * half + 128]

            @pl.when(place[5] == half)
            def _():
                kept[...] = rows

            @pl.when(place[5] != half)
            def _():
                sent[...] = rows.astype(BF16)

    contract = (((0,), (0,)), ((), ()))
    gate_term = lax.dot_general(x, grad_gate, contract, preferred_element_type=F32)
    up_term = lax.dot_general(x, grad_up, contract, preferred_element_type=F32)

    @pl.when(step == 0)
    def _():
        grads[0], grads[1] = gate_term, up_term

    @pl.when(step > 0)
    def _():
        grads[0] += gate_term
        grads[1] += up_term

    @pl.when(step == steps - 1)
    def _():
        for k, ref in enumerate((own, p1, p2, p3)):
            block = lax.rem(place[0] + k, 4)
            for s in range(8):
                row = block * place[2] + (s // 2) * place[3] + (s % 2) * 64
                for which in range(2):
                    value = grads[which, pl.ds(pl.multiple_of(row, 16), 16), :] * scale
                    ref[which, s * 16 : s * 16 + 16, :] = value.astype(ref.dtype)


def main(place, coeffs, cores, hidden, before, start, cols, scale):
    tokens, rank = coeffs.shape
    tile = 256
    first = before is None
    whole = pl.BlockSpec((2, 128, cols), lambda i: (0, 0, 0))
    row_block = pl.BlockSpec((tile, rank), lambda i: (i, 0))
    half_block = pl.BlockSpec((tile // 2, rank), lambda i: (i, 0))
    if first:
        outs, specs = [like(tokens, rank, kind=F32)], [row_block]
    else:
        outs = [like(tokens // 2, rank, kind=F32), like(tokens // 2, rank)]
        specs = [half_block] * 2
    return pl.pallas_call(
        functools.partial(main_body, scale, start),
        grid=(tokens // tile,),
        out_shape=outs + [like(2, 128, cols, kind=F32)] + [like(2, 128, cols)] * 3,
        in_specs=[SMEM, row_block]
        + [whole] * 4
        + [HBM]
        + ([] if first else [row_block]),
        out_specs=specs + [whole] * 4,
        scratch_shapes=[
            pltpu.VMEM((2, rank, cols), BF16),
            pltpu.VMEM((2, rank, cols), F32),
            pltpu.VMEM((tokens // tile, tile, cols), BF16),
            pltpu.SemaphoreType.DMA((tokens // tile,)),
        ],
        compiler_params=pltpu.CompilerParams(vmem_limit_bytes=32 * MIB),
        cost_estimate=pl.CostEstimate(
            flops=12 * tokens * rank * cols,
            bytes_accessed=10 * MIB,
            transcendentals=tokens * cols,
        ),
        name="main",
    )(place, coeffs, *cores, hidden, *([] if first else [before]))


def halve_body(place, own, r1, r2, r3, kept, sent):
    for ref, half in ((kept, place[4]), (sent, 1 - place[4])):
        at = (slice(None), pl.ds(pl.multiple_of(half * 16, 16), 16), slice(None))
        ref[...] = add4(own, r1, r2, r3, at).astype(ref.dtype)


def last_body(place, own, got, *refs):
    tokens, gate, up = refs[-3:]
    tokens[...] = (own[...] + got[...].astype(F32)).astype(BF16)
    first = 0
    for kept, got in zip(refs[:-3:2], refs[1:-3:2]):
        cols = slice(first, first + kept.shape[2])
        gate[:, cols] = kept[0] + got[0].astype(F32)
        up[:, cols] = kept[1] + got[1].astype(F32)
        first += kept.shape[2]


def tokens_body(place, total, got, kept, sent):
    for ref, flip in ((kept, 0), (sent, 1)):
        for i in range(2):
            block = place[6] ^ (flip + 2 * i)
            at = (pl.ds(pl.multiple_of(block * 128, 128), 128), slice(None))
            value = total[at] + got[at].astype(F32)
            ref[128 * i : 128 * i + 128, :] = value.astype(ref.dtype)


def tokens_half_body(place, total, got, kept, sent):
    kept[...] = total[:128] + got[:128].astype(F32)
    sent[...] = (total[128:] + got[128:].astype(F32)).astype(BF16)


def scatter_tokens(place, kept, sent):
    rank = kept.shape[1]
    got = lax.ppermute(sent, "tensor", SWAP_CORE)
    for size, body, name in ((256, tokens_body, "tokens"), (128, tokens_half_body, "tokens_half")):
        outs = [like(size, rank, kind=F32), like(size, rank)]
        kept, sent = call(body, outs, (place, kept, got), name=name)
        got = lax.ppermute(sent, "tensor", SWAP_LOW[size == 128])
    return [kept, got]


def local(coeffs, pca_basis, w_gate, w_up, grad_hidden):
    fsdp, tensor = lax.axis_index("fsdp"), lax.axis_index("tensor")
    core, low = tensor & 1, tensor >> 1
    x, z, y = fsdp >> 3, (fsdp >> 2) & 1, fsdp & 3
    a, b = jnp.where(core == 0, y, x), jnp.where(core == 0, x, y)
    stride_a, stride_b = jnp.where(core == 0, 16, 128), jnp.where(core == 0, 128, 16)
    place = jnp.stack([a, b, stride_a, stride_b, z, core, low]).astype(jnp.int32)
    width = w_gate.shape[1]
    scale = 1.0 / math.sqrt(coeffs.shape[0] * 32)
    starts = [sum(WIDTHS[:c]) for c in range(len(WIDTHS))]

    own, *pieces = partial_cores(place, pca_basis, w_gate, w_up)
    halves, cores = [], []
    for cols, (own, *pieces) in zip(WIDTHS, relay(place, own, pieces, WIDTHS)):
        ins = (place, own, *send(pieces, "b"))
        halves.append(call(sum4_body, like(2, 32, cols), ins, name="sum4"))
    for cols, half in zip(WIDTHS, halves):
        ins = (place, half, swap_z(half))
        cores.append(call(add2_body, like(2, 32, cols), ins, halves[-1:], name="add2"))
    ins = [place]
    for core in cores:
        ins += [core] + send([core] * 3, "b")
    blocks = call(join_body, [like(2, 128, cols) for cols in WIDTHS], ins, name="join")
    cores = [[block] + send([block] * 3, "a") for block in blocks]
    total, grads = [None], []
    for start, cols, core in zip(starts, WIDTHS, cores):
        *total, own, p1, p2, p3 = main(
            place, coeffs, core, grad_hidden, total[0], start, cols, scale
        )
        grads.append((own, p1, p2, p3))
    own, *pieces = grads[0]
    parts = list(relay(place, own, pieces, WIDTHS[:1], total[:1])[0])
    tokens = scatter_tokens(place, *total)
    own, *pieces = grads[1]
    parts += [own] + send(pieces, "a")
    outs = [like(2, 32, width, kind=F32)] + [like(2, 32, width)] * 3
    own, *pieces = call(regroup_body, outs, (place, *parts), tokens[:1], name="regroup")
    outs = [like(2, 16, width, kind=F32), like(2, 16, width)]
    kept, sent = call(halve_body, outs, (place, own, *send(pieces, "b")), name="halve")
    ends = [kept, swap_z(sent)]
    outs = [like(*tokens[0].shape), like(16, width, kind=F32), like(16, width, kind=F32)]
    return call(last_body, outs, (place, *tokens, *ends), name="last")


def solution(mesh):
    placed = (
        P("fsdp", None),
        P("fsdp", None),
        P("fsdp", "tensor"),
        P("fsdp", "tensor"),
        P("fsdp", "tensor"),
    )
    return jax.shard_map(
        local,
        mesh=mesh,
        in_specs=placed,
        out_specs=(P(BOTH, None), P("fsdp", "tensor"), P("fsdp", "tensor")),
        check_vma=False,
    )
```

```python
import functools
import math

import jax
import jax.numpy as jnp
from jax import lax
from jax.experimental import pallas as pl
from jax.experimental.pallas import tpu as pltpu
from jax.sharding import PartitionSpec as P

BF16, F32 = jnp.bfloat16, jnp.float32
BOTH = ("fsdp", "tensor")
WIDTHS = (896, 896)
MIB = 1 << 20
SLICES = 4
K1_LIMIT = 58
SMEM = pl.BlockSpec(memory_space=pltpu.SMEM)
VMEM = pl.BlockSpec(memory_space=pltpu.VMEM)
ANY = pl.BlockSpec(memory_space=pl.ANY)
HBM = pl.BlockSpec(memory_space=pltpu.HBM)
PLACES = [(x, z, y, t) for x in range(4) for z in range(2) for y in range(4) for t in range(8)]


def index(x, z, y, t):
    return (x * 8 + z * 4 + y) * 8 + t


def along_y(t, ring):
    return (t % 2 == 0) == (ring == "a")


def shift(ring, k):
    pairs = []
    for x, z, y, t in PLACES:
        u, v = (x, (y + k) % 4) if along_y(t, ring) else ((x + k) % 4, y)
        pairs.append((index(x, z, y, t), index(u, z, v, t)))
    return pairs


SHIFTS = {ring: [shift(ring, k) for k in (1, 2, 3)] for ring in "ab"}
SWAP_Z = [(index(x, z, y, t), index(x, 1 - z, y, t)) for x, z, y, t in PLACES]


def send(pieces, ring):
    return [lax.ppermute(piece, BOTH, SHIFTS[ring][k]) for k, piece in enumerate(pieces)]


def swap_z(piece):
    return lax.ppermute(piece, BOTH, SWAP_Z)


def like(*shape, kind=BF16):
    return jax.ShapeDtypeStruct(shape, kind)


def call(body, out_shape, ins, after=(), limit=16, moved=MIB, name=None):
    n, skip = len(ins), len(after)

    def kernel(*refs):
        body(*refs[:n], *refs[n + skip :])

    return pl.pallas_call(
        kernel,
        out_shape=out_shape,
        in_specs=[SMEM] + [VMEM] * (n - 1) + [ANY] * skip,
        out_specs=jax.tree.map(lambda _: VMEM, out_shape),
        compiler_params=pltpu.CompilerParams(vmem_limit_bytes=limit * MIB),
        cost_estimate=pl.CostEstimate(flops=0, bytes_accessed=moved, transcendentals=0),
        name=name,
    )(*ins, *after)


def cores_body(place, basis_hbm, gate_hbm, up_hbm, own, p1, p2, p3, basis, weights, sems):
    depth = basis.shape[0]
    rows = depth // SLICES
    copies = [pltpu.make_async_copy(basis_hbm, basis, sems.at[2 * SLICES])]
    for which, source in enumerate((gate_hbm, up_hbm)):
        for i in range(SLICES):
            at = pl.ds(i * rows, rows)
            sem = sems.at[which * SLICES + i]
            copies.append(pltpu.make_async_copy(source.at[at, :], weights.at[which, at, :], sem))
    for copy in copies:
        copy.start()
    copies[0].wait()
    contract = (((0,), (0,)), ((), ()))
    for which in range(2):
        for copy in copies[1 + which * SLICES : 1 + which * SLICES + SLICES]:
            copy.wait()
        for k, ref in ((2, p2), (1, p1), (3, p3), (0, own)):
            block = lax.rem(place[0] + k, 4)
            part = basis[:, pl.ds(pl.multiple_of(block * 128, 128), 128)]
            total = lax.dot_general(part, weights[which], contract, preferred_element_type=F32)
            ref[which] = total.astype(ref.dtype)


def partial_cores(place, basis, w_gate, w_up):
    depth, width = w_gate.shape
    return pl.pallas_call(
        cores_body,
        out_shape=[like(2, 128, width)] * 4,
        in_specs=[SMEM, HBM, HBM, HBM],
        out_specs=[VMEM] * 4,
        scratch_shapes=[
            pltpu.VMEM(basis.shape, BF16),
            pltpu.VMEM((2, depth, width), BF16),
            pltpu.SemaphoreType.DMA((2 * SLICES + 1,)),
        ],
        compiler_params=pltpu.CompilerParams(vmem_limit_bytes=K1_LIMIT * MIB),
        cost_estimate=pl.CostEstimate(
            flops=4 * depth * basis.shape[1] * width, bytes_accessed=6 * MIB, transcendentals=0
        ),
        name="partial_cores",
    )(place, basis, w_gate, w_up)


def add4(own, r1, r2, r3, at):
    return (own[at].astype(F32) + r1[at].astype(F32)) + (r2[at].astype(F32) + r3[at].astype(F32))


def relay_body(place, own, r1, r2, r3, *outs):
    for k in range(4):
        rows = pl.ds(pl.multiple_of(lax.rem(place[1] + k, 4) * 32, 32), 32)
        first = 0
        for ref in outs[k::4]:
            at = (slice(None), rows, slice(first, first + ref.shape[2]))
            ref[...] = add4(own, r1, r2, r3, at).astype(ref.dtype)
            first += ref.shape[2]


def relay(place, own, pieces, widths, after=()):
    outs = []
    for cols in widths:
        outs += [like(2, 32, cols, kind=F32)] + [like(2, 32, cols)] * 3
    outs = call(relay_body, outs, (place, own, *send(pieces, "a")), after, name="relay")
    return [outs[4 * c : 4 * c + 4] for c in range(len(widths))]


def regroup_body(place, c0, c1, c2, c3, own, r1, r2, r3, *outs):
    first = c0.shape[2]
    for k, (before, ref) in enumerate(zip((c0, c1, c2, c3), outs)):
        rows = pl.ds(pl.multiple_of(lax.rem(place[1] + k, 4) * 32, 32), 32)
        value = add4(own, r1, r2, r3, (slice(None), rows, slice(None)))
        ref[:, :, :first] = before[...]
        ref[:, :, first:] = value.astype(ref.dtype)


def sum4_body(place, own, r1, r2, r3, out):
    out[...] = add4(own, r1, r2, r3, ...).astype(out.dtype)


def add2_body(place, a, b, out):
    out[...] = (a[...].astype(F32) + b[...].astype(F32)).astype(BF16)


def join_body(place, *refs):
    outs = refs[len(refs) // 5 * 4 :]
    for chunk, out in enumerate(outs):
        for k, ref in enumerate(refs[4 * chunk : 4 * chunk + 4]):
            at = pl.ds(pl.multiple_of(lax.rem(place[1] + 4 - k, 4) * 32, 32), 32)
            out[:, at, :] = ref[...]


def main_body(scale, start, place, coeffs, c0, c1, c2, c3, hidden_hbm, *rest):
    first = start == 0
    if first:
        dcoeffs, own, p1, p2, p3, core, grads, terms, hidden, sems = rest
    else:
        before, dcoeffs, own, p1, p2, p3, core, grads, terms, hidden, sems = rest
    tiles, tile, cols = hidden.shape
    copies = []
    for i in range(tiles):
        source = hidden_hbm.at[pl.ds(i * tile, tile), pl.ds(start, cols)]
        copies.append(pltpu.make_async_copy(source, hidden.at[i], sems.at[i]))
        copies[i].start()
    for k, ref in enumerate((c0, c1, c2, c3)):
        at = pl.multiple_of(lax.rem(place[0] + 4 - k, 4) * 128, 128)
        core[:, pl.ds(at, 128), :] = ref[...]

    for i in range(tiles):
        rows = slice(i * tile, i * tile + tile)
        x = coeffs[rows, :]
        gate = jnp.dot(x, core[0], preferred_element_type=F32)
        upward = jnp.dot(x, core[1], preferred_element_type=F32)
        sig = 0.5 * jnp.tanh(0.5 * gate) + 0.5
        copies[i].wait()
        scaled = hidden[i].astype(F32) * sig
        terms[0, rows, :] = (scaled * upward * (1.0 + gate * (1.0 - sig))).astype(BF16)
        terms[1, rows, :] = (scaled * gate).astype(BF16)
        contract = (((1,), (1,)), ((), ()))
        total = lax.dot_general(terms[0, rows, :], core[0], contract, preferred_element_type=F32)
        total += lax.dot_general(terms[1, rows, :], core[1], contract, preferred_element_type=F32)
        if not first:
            total += before[rows, :]
        dcoeffs[rows, :] = total.astype(dcoeffs.dtype)

    contract = (((0,), (0,)), ((), ()))
    for which in range(2):
        grads[which] = lax.dot_general(
            coeffs[...], terms[which], contract, preferred_element_type=F32
        )
    for k, ref in enumerate((own, p1, p2, p3)):
        block = lax.rem(place[0] + k, 4)
        for s in range(8):
            row = block * place[2] + (s // 2) * place[3] + (s % 2) * 64
            for which in range(2):
                value = grads[which, pl.ds(pl.multiple_of(row, 16), 16), :] * scale
                ref[which, s * 16 : s * 16 + 16, :] = value.astype(ref.dtype)


def main(place, coeffs, cores, hidden, before, start, cols, scale):
    tokens, rank = coeffs.shape
    tile = 256
    first = before is None
    outs = [like(tokens, rank, kind=F32 if first else BF16)]
    outs += [like(2, 128, cols, kind=F32)] + [like(2, 128, cols)] * 3
    return pl.pallas_call(
        functools.partial(main_body, scale, start),
        out_shape=outs,
        in_specs=[SMEM] + [VMEM] * 5 + [HBM] + ([] if first else [VMEM]),
        out_specs=[VMEM] * len(outs),
        scratch_shapes=[
            pltpu.VMEM((2, rank, cols), BF16),
            pltpu.VMEM((2, rank, cols), F32),
            pltpu.VMEM((2, tokens, cols), BF16),
            pltpu.VMEM((tokens // tile, tile, cols), BF16),
            pltpu.SemaphoreType.DMA((tokens // tile,)),
        ],
        compiler_params=pltpu.CompilerParams(vmem_limit_bytes=24 * MIB),
        cost_estimate=pl.CostEstimate(
            flops=12 * tokens * rank * cols,
            bytes_accessed=10 * MIB,
            transcendentals=tokens * cols,
        ),
        name="main",
    )(place, coeffs, *cores, hidden, *([] if first else [before]))


def halve_body(place, own, r1, r2, r3, kept, sent):
    for ref, half in ((kept, place[4]), (sent, 1 - place[4])):
        at = (slice(None), pl.ds(pl.multiple_of(half * 16, 16), 16), slice(None))
        ref[...] = add4(own, r1, r2, r3, at).astype(ref.dtype)


def last_body(place, kept, got, gate, up):
    gate[...] = kept[0] + got[0].astype(F32)
    up[...] = kept[1] + got[1].astype(F32)


def tokens_body(place, got, out):
    n = out.shape[0]
    total = got[:n].astype(F32)
    for i in range(1, got.shape[0] // n):
        total += got[i * n : i * n + n].astype(F32)
    out[...] = total.astype(BF16)


def local(coeffs, pca_basis, w_gate, w_up, grad_hidden):
    fsdp, tensor = lax.axis_index("fsdp"), lax.axis_index("tensor")
    core, low = tensor & 1, tensor >> 1
    x, z, y = fsdp >> 3, (fsdp >> 2) & 1, fsdp & 3
    a, b = jnp.where(core == 0, y, x), jnp.where(core == 0, x, y)
    stride_a, stride_b = jnp.where(core == 0, 16, 128), jnp.where(core == 0, 128, 16)
    place = jnp.stack([a, b, stride_a, stride_b, z, core, low]).astype(jnp.int32)
    width = w_gate.shape[1]
    scale = 1.0 / math.sqrt(coeffs.shape[0] * 32)
    starts = [sum(WIDTHS[:c]) for c in range(len(WIDTHS))]

    own, *pieces = partial_cores(place, pca_basis, w_gate, w_up)
    halves, cores = [], []
    for cols, (own, *pieces) in zip(WIDTHS, relay(place, own, pieces, WIDTHS)):
        ins = (place, own, *send(pieces, "b"))
        halves.append(call(sum4_body, like(2, 32, cols), ins, name="sum4"))
    for cols, half in zip(WIDTHS, halves):
        ins = (place, half, swap_z(half))
        cores.append(call(add2_body, like(2, 32, cols), ins, halves[-1:], name="add2"))
    ins = [place]
    for core in cores:
        ins += [core] + send([core] * 3, "b")
    blocks = call(join_body, [like(2, 128, cols) for cols in WIDTHS], ins, name="join")
    cores = [[block] + send([block] * 3, "a") for block in blocks]
    total, grads = [None], []
    for start, cols, core in zip(starts, WIDTHS, cores):
        *total, own, p1, p2, p3 = main(
            place, coeffs, core, grad_hidden, total[0], start, cols, scale
        )
        grads.append((own, p1, p2, p3))
    own, *pieces = grads[0]
    parts = list(relay(place, own, pieces, WIDTHS[:1], total[:1])[0])
    ready, _ = lax.optimization_barrier((total[0], parts[0]))
    got = lax.all_to_all(ready, "tensor", 0, 0, tiled=True)
    own, *pieces = grads[1]
    parts += [own] + send(pieces, "a")
    outs = [like(2, 32, width, kind=F32)] + [like(2, 32, width)] * 3
    own, *pieces = call(regroup_body, outs, (place, *parts), name="regroup")
    outs = [like(2, 16, width, kind=F32), like(2, 16, width)]
    kept, sent = call(halve_body, outs, (place, own, *send(pieces, "b")), name="halve")
    tokens = like(got.shape[0] // lax.axis_size("tensor"), got.shape[1])
    tokens = call(tokens_body, tokens, (place, got), (kept,), name="tokens")
    outs = [like(16, width, kind=F32)] * 2
    ends = (place, kept, swap_z(sent))
    return tokens, *call(last_body, outs, ends, (tokens,), name="last")


def solution(mesh):
    placed = (
        P("fsdp", None),
        P("fsdp", None),
        P("fsdp", "tensor"),
        P("fsdp", "tensor"),
        P("fsdp", "tensor"),
    )
    return jax.shard_map(
        local,
        mesh=mesh,
        in_specs=placed,
        out_specs=(P(BOTH, None), P("fsdp", "tensor"), P("fsdp", "tensor")),
        check_vma=False,
    )
```

```python
import functools
import math

import jax
import jax.numpy as jnp
from jax import lax
from jax.experimental import pallas as pl
from jax.experimental.pallas import tpu as pltpu
from jax.sharding import PartitionSpec as P

BF16, F32 = jnp.bfloat16, jnp.float32
BOTH = ("fsdp", "tensor")
WIDTHS = (896, 896)
MIB = 1 << 20
SLICES = 4
K1_LIMIT = 58
SMEM = pl.BlockSpec(memory_space=pltpu.SMEM)
VMEM = pl.BlockSpec(memory_space=pltpu.VMEM)
ANY = pl.BlockSpec(memory_space=pl.ANY)
HBM = pl.BlockSpec(memory_space=pltpu.HBM)
PLACES = [(x, z, y, t) for x in range(4) for z in range(2) for y in range(4) for t in range(8)]


def index(x, z, y, t):
    return (x * 8 + z * 4 + y) * 8 + t


def along_y(t, ring):
    return (t % 2 == 0) == (ring == "a")


def shift(ring, k):
    pairs = []
    for x, z, y, t in PLACES:
        u, v = (x, (y + k) % 4) if along_y(t, ring) else ((x + k) % 4, y)
        pairs.append((index(x, z, y, t), index(u, z, v, t)))
    return pairs


SHIFTS = {ring: [shift(ring, k) for k in (1, 2, 3)] for ring in "ab"}
SWAP_Z = [(index(x, z, y, t), index(x, 1 - z, y, t)) for x, z, y, t in PLACES]
SWAP_CORE = [(t, t ^ 1) for t in range(8)]
SWAP_LOW = [[(t, t ^ 2 * bit) for t in range(8)] for bit in (1, 2)]


def send(pieces, ring):
    return [lax.ppermute(piece, BOTH, SHIFTS[ring][k]) for k, piece in enumerate(pieces)]


def swap_z(piece):
    return lax.ppermute(piece, BOTH, SWAP_Z)


def like(*shape, kind=BF16):
    return jax.ShapeDtypeStruct(shape, kind)


def call(body, out_shape, ins, after=(), limit=16, moved=MIB, name=None):
    n, skip = len(ins), len(after)

    def kernel(*refs):
        body(*refs[:n], *refs[n + skip :])

    return pl.pallas_call(
        kernel,
        out_shape=out_shape,
        in_specs=[SMEM] + [VMEM] * (n - 1) + [ANY] * skip,
        out_specs=jax.tree.map(lambda _: VMEM, out_shape),
        compiler_params=pltpu.CompilerParams(vmem_limit_bytes=limit * MIB),
        cost_estimate=pl.CostEstimate(flops=0, bytes_accessed=moved, transcendentals=0),
        name=name,
    )(*ins, *after)


def cores_body(place, basis_hbm, gate_hbm, up_hbm, own, p1, p2, p3, basis, weights, sems):
    depth = basis.shape[0]
    rows = depth // SLICES
    copies = [pltpu.make_async_copy(basis_hbm, basis, sems.at[2 * SLICES])]
    for which, source in enumerate((gate_hbm, up_hbm)):
        for i in range(SLICES):
            at = pl.ds(i * rows, rows)
            sem = sems.at[which * SLICES + i]
            copies.append(pltpu.make_async_copy(source.at[at, :], weights.at[which, at, :], sem))
    for copy in copies:
        copy.start()
    copies[0].wait()
    contract = (((0,), (0,)), ((), ()))
    for which in range(2):
        for copy in copies[1 + which * SLICES : 1 + which * SLICES + SLICES]:
            copy.wait()
        for k, ref in ((2, p2), (1, p1), (3, p3), (0, own)):
            block = lax.rem(place[0] + k, 4)
            part = basis[:, pl.ds(pl.multiple_of(block * 128, 128), 128)]
            total = lax.dot_general(part, weights[which], contract, preferred_element_type=F32)
            ref[which] = total.astype(ref.dtype)


def partial_cores(place, basis, w_gate, w_up):
    depth, width = w_gate.shape
    return pl.pallas_call(
        cores_body,
        out_shape=[like(2, 128, width)] * 4,
        in_specs=[SMEM, HBM, HBM, HBM],
        out_specs=[VMEM] * 4,
        scratch_shapes=[
            pltpu.VMEM(basis.shape, BF16),
            pltpu.VMEM((2, depth, width), BF16),
            pltpu.SemaphoreType.DMA((2 * SLICES + 1,)),
        ],
        compiler_params=pltpu.CompilerParams(vmem_limit_bytes=K1_LIMIT * MIB),
        cost_estimate=pl.CostEstimate(
            flops=4 * depth * basis.shape[1] * width, bytes_accessed=6 * MIB, transcendentals=0
        ),
        name="partial_cores",
    )(place, basis, w_gate, w_up)


def add4(own, r1, r2, r3, at):
    return (own[at].astype(F32) + r1[at].astype(F32)) + (r2[at].astype(F32) + r3[at].astype(F32))


def relay_body(place, own, r1, r2, r3, *outs):
    for k in range(4):
        rows = pl.ds(pl.multiple_of(lax.rem(place[1] + k, 4) * 32, 32), 32)
        first = 0
        for ref in outs[k::4]:
            at = (slice(None), rows, slice(first, first + ref.shape[2]))
            ref[...] = add4(own, r1, r2, r3, at).astype(ref.dtype)
            first += ref.shape[2]


def relay(place, own, pieces, widths, after=()):
    outs = []
    for cols in widths:
        outs += [like(2, 32, cols, kind=F32)] + [like(2, 32, cols)] * 3
    outs = call(relay_body, outs, (place, own, *send(pieces, "a")), after, name="relay")
    return [outs[4 * c : 4 * c + 4] for c in range(len(widths))]


def regroup_body(place, c0, c1, c2, c3, own, r1, r2, r3, *outs):
    first = c0.shape[2]
    for k, (before, ref) in enumerate(zip((c0, c1, c2, c3), outs)):
        rows = pl.ds(pl.multiple_of(lax.rem(place[1] + k, 4) * 32, 32), 32)
        value = add4(own, r1, r2, r3, (slice(None), rows, slice(None)))
        ref[:, :, :first] = before[...]
        ref[:, :, first:] = value.astype(ref.dtype)


def sum4_body(place, own, r1, r2, r3, out):
    out[...] = add4(own, r1, r2, r3, ...).astype(out.dtype)


def add2_body(place, a, b, out):
    out[...] = (a[...].astype(F32) + b[...].astype(F32)).astype(BF16)


def join_body(place, *refs):
    outs = refs[len(refs) // 5 * 4 :]
    for chunk, out in enumerate(outs):
        for k, ref in enumerate(refs[4 * chunk : 4 * chunk + 4]):
            at = pl.ds(pl.multiple_of(lax.rem(place[1] + 4 - k, 4) * 32, 32), 32)
            out[:, at, :] = ref[...]


def main_body(scale, start, place, coeffs, c0, c1, c2, c3, hidden_hbm, *rest):
    first = start == 0
    if first:
        dcoeffs, own, p1, p2, p3, core, grads, terms, hidden, sems = rest
    else:
        before, kept, sent, own, p1, p2, p3, core, grads, terms, hidden, sems = rest
    tiles, tile, cols = hidden.shape
    copies = []
    for i in range(tiles):
        source = hidden_hbm.at[pl.ds(i * tile, tile), pl.ds(start, cols)]
        copies.append(pltpu.make_async_copy(source, hidden.at[i], sems.at[i]))
        copies[i].start()
    for k, ref in enumerate((c0, c1, c2, c3)):
        at = pl.multiple_of(lax.rem(place[0] + 4 - k, 4) * 128, 128)
        core[:, pl.ds(at, 128), :] = ref[...]

    for i in range(tiles):
        rows = slice(i * tile, i * tile + tile)
        x = coeffs[rows, :]
        gate = jnp.dot(x, core[0], preferred_element_type=F32)
        upward = jnp.dot(x, core[1], preferred_element_type=F32)
        sig = 0.5 * jnp.tanh(0.5 * gate) + 0.5
        copies[i].wait()
        scaled = hidden[i].astype(F32) * sig
        terms[0, rows, :] = (scaled * upward * (1.0 + gate * (1.0 - sig))).astype(BF16)
        terms[1, rows, :] = (scaled * gate).astype(BF16)
        contract = (((1,), (1,)), ((), ()))
        total = lax.dot_general(terms[0, rows, :], core[0], contract, preferred_element_type=F32)
        total += lax.dot_general(terms[1, rows, :], core[1], contract, preferred_element_type=F32)
        if first:
            dcoeffs[rows, :] = total
            continue
        total += before[rows, :]
        size = tile // 2
        out_rows = slice(i * size, i * size + size)
        for half in range(2):
            value = total[size * half : size * half + size]

            @pl.when(place[5] == half)
            def _():
                kept[out_rows, :] = value

            @pl.when(place[5] != half)
            def _():
                sent[out_rows, :] = value.astype(BF16)

    contract = (((0,), (0,)), ((), ()))
    for which in range(2):
        grads[which] = lax.dot_general(
            coeffs[...], terms[which], contract, preferred_element_type=F32
        )
    for k, ref in enumerate((own, p1, p2, p3)):
        block = lax.rem(place[0] + k, 4)
        for s in range(8):
            row = block * place[2] + (s // 2) * place[3] + (s % 2) * 64
            for which in range(2):
                value = grads[which, pl.ds(pl.multiple_of(row, 16), 16), :] * scale
                ref[which, s * 16 : s * 16 + 16, :] = value.astype(ref.dtype)


def main(place, coeffs, cores, hidden, before, start, cols, scale):
    tokens, rank = coeffs.shape
    tile = 256
    first = before is None
    if first:
        outs = [like(tokens, rank, kind=F32)]
    else:
        outs = [like(tokens // 2, rank, kind=F32), like(tokens // 2, rank)]
    outs += [like(2, 128, cols, kind=F32)] + [like(2, 128, cols)] * 3
    return pl.pallas_call(
        functools.partial(main_body, scale, start),
        out_shape=outs,
        in_specs=[SMEM] + [VMEM] * 5 + [HBM] + ([] if first else [VMEM]),
        out_specs=[VMEM] * len(outs),
        scratch_shapes=[
            pltpu.VMEM((2, rank, cols), BF16),
            pltpu.VMEM((2, rank, cols), F32),
            pltpu.VMEM((2, tokens, cols), BF16),
            pltpu.VMEM((tokens // tile, tile, cols), BF16),
            pltpu.SemaphoreType.DMA((tokens // tile,)),
        ],
        compiler_params=pltpu.CompilerParams(vmem_limit_bytes=24 * MIB),
        cost_estimate=pl.CostEstimate(
            flops=12 * tokens * rank * cols,
            bytes_accessed=10 * MIB,
            transcendentals=tokens * cols,
        ),
        name="main",
    )(place, coeffs, *cores, hidden, *([] if first else [before]))


def halve_body(place, own, r1, r2, r3, kept, sent):
    for ref, half in ((kept, place[4]), (sent, 1 - place[4])):
        at = (slice(None), pl.ds(pl.multiple_of(half * 16, 16), 16), slice(None))
        ref[...] = add4(own, r1, r2, r3, at).astype(ref.dtype)


def last_body(place, own, other, kept, got, tokens, gate, up):
    tokens[...] = (own[...] + other[...].astype(F32)).astype(BF16)
    gate[...] = kept[0] + got[0].astype(F32)
    up[...] = kept[1] + got[1].astype(F32)


def tokens_body(place, total, got, kept, sent):
    for ref, flip in ((kept, 0), (sent, 1)):
        for i in range(2):
            block = place[6] ^ (flip + 2 * i)
            at = (pl.ds(pl.multiple_of(block * 128, 128), 128), slice(None))
            value = total[at] + got[at].astype(F32)
            ref[128 * i : 128 * i + 128, :] = value.astype(ref.dtype)


def tokens_half_body(place, total, got, kept, sent):
    kept[...] = total[:128] + got[:128].astype(F32)
    sent[...] = (total[128:] + got[128:].astype(F32)).astype(BF16)


def scatter_tokens(place, kept, sent, after):
    rank = kept.shape[1]
    got = lax.ppermute(sent, "tensor", SWAP_CORE)
    for size, body, name in ((256, tokens_body, "tokens"), (128, tokens_half_body, "tokens_half")):
        outs = [like(size, rank, kind=F32), like(size, rank)]
        kept, sent = call(body, outs, (place, kept, got), after, name=name)
        got = lax.ppermute(sent, "tensor", SWAP_LOW[size == 128])
    return kept, got


def local(coeffs, pca_basis, w_gate, w_up, grad_hidden):
    fsdp, tensor = lax.axis_index("fsdp"), lax.axis_index("tensor")
    core, low = tensor & 1, tensor >> 1
    x, z, y = fsdp >> 3, (fsdp >> 2) & 1, fsdp & 3
    a, b = jnp.where(core == 0, y, x), jnp.where(core == 0, x, y)
    stride_a, stride_b = jnp.where(core == 0, 16, 128), jnp.where(core == 0, 128, 16)
    place = jnp.stack([a, b, stride_a, stride_b, z, core, low]).astype(jnp.int32)
    width = w_gate.shape[1]
    scale = 1.0 / math.sqrt(coeffs.shape[0] * 32)
    starts = [sum(WIDTHS[:c]) for c in range(len(WIDTHS))]

    own, *pieces = partial_cores(place, pca_basis, w_gate, w_up)
    halves, cores = [], []
    for cols, (own, *pieces) in zip(WIDTHS, relay(place, own, pieces, WIDTHS)):
        ins = (place, own, *send(pieces, "b"))
        halves.append(call(sum4_body, like(2, 32, cols), ins, name="sum4"))
    for cols, half in zip(WIDTHS, halves):
        ins = (place, half, swap_z(half))
        cores.append(call(add2_body, like(2, 32, cols), ins, halves[-1:], name="add2"))
    ins = [place]
    for core in cores:
        ins += [core] + send([core] * 3, "b")
    blocks = call(join_body, [like(2, 128, cols) for cols in WIDTHS], ins, name="join")
    cores = [[block] + send([block] * 3, "a") for block in blocks]
    total, grads = [None], []
    for start, cols, core in zip(starts, WIDTHS, cores):
        *total, own, p1, p2, p3 = main(
            place, coeffs, core, grad_hidden, total[0], start, cols, scale
        )
        grads.append((own, p1, p2, p3))
    own, *pieces = grads[0]
    parts = list(relay(place, own, pieces, WIDTHS[:1], total[:1])[0])
    kept, sent = total
    sent, _ = lax.optimization_barrier((sent, parts[0]))
    tokens, other = scatter_tokens(place, kept, sent, ())
    own, *pieces = grads[1]
    parts += [own] + send(pieces, "a")
    outs = [like(2, 32, width, kind=F32)] + [like(2, 32, width)] * 3
    own, *pieces = call(regroup_body, outs, (place, *parts), (tokens,), name="regroup")
    outs = [like(2, 16, width, kind=F32), like(2, 16, width)]
    kept, sent = call(halve_body, outs, (place, own, *send(pieces, "b")), name="halve")
    ends = [kept, swap_z(sent)]
    outs = [like(*tokens.shape)] + [like(16, width, kind=F32)] * 2
    return call(last_body, outs, (place, tokens, other, *ends), name="last")


def solution(mesh):
    placed = (
        P("fsdp", None),
        P("fsdp", None),
        P("fsdp", "tensor"),
        P("fsdp", "tensor"),
        P("fsdp", "tensor"),
    )
    return jax.shard_map(
        local,
        mesh=mesh,
        in_specs=placed,
        out_specs=(P(BOTH, None), P("fsdp", "tensor"), P("fsdp", "tensor")),
        check_vma=False,
    )
```

```python
import functools
import math

import jax
import jax.numpy as jnp
from jax import lax
from jax.experimental import pallas as pl
from jax.experimental.pallas import tpu as pltpu
from jax.sharding import PartitionSpec as P

BF16, F32 = jnp.bfloat16, jnp.float32
BOTH = ("fsdp", "tensor")
WIDTHS = (896, 896)
MIB = 1 << 20
SLICES = 4
K1_LIMIT = 58
SMEM = pl.BlockSpec(memory_space=pltpu.SMEM)
VMEM = pl.BlockSpec(memory_space=pltpu.VMEM)
ANY = pl.BlockSpec(memory_space=pl.ANY)
HBM = pl.BlockSpec(memory_space=pltpu.HBM)
PLACES = [(x, z, y, t) for x in range(4) for z in range(2) for y in range(4) for t in range(8)]


def index(x, z, y, t):
    return (x * 8 + z * 4 + y) * 8 + t


def along_y(t, ring):
    return (t % 2 == 0) == (ring == "a")


def shift(ring, k):
    pairs = []
    for x, z, y, t in PLACES:
        u, v = (x, (y + k) % 4) if along_y(t, ring) else ((x + k) % 4, y)
        pairs.append((index(x, z, y, t), index(u, z, v, t)))
    return pairs


SHIFTS = {ring: [shift(ring, k) for k in (1, 2, 3)] for ring in "ab"}
SWAP_Z = [(index(x, z, y, t), index(x, 1 - z, y, t)) for x, z, y, t in PLACES]
SWAP_CORE = [(t, t ^ 1) for t in range(8)]
SWAP_LOW = [[(t, t ^ 2 * bit) for t in range(8)] for bit in (1, 2)]


def send(pieces, ring):
    return [lax.ppermute(piece, BOTH, SHIFTS[ring][k]) for k, piece in enumerate(pieces)]


def swap_z(piece):
    return lax.ppermute(piece, BOTH, SWAP_Z)


def like(*shape, kind=BF16):
    return jax.ShapeDtypeStruct(shape, kind)


def call(body, out_shape, ins, after=(), limit=16, moved=MIB, name=None):
    n, skip = len(ins), len(after)

    def kernel(*refs):
        body(*refs[:n], *refs[n + skip :])

    return pl.pallas_call(
        kernel,
        out_shape=out_shape,
        in_specs=[SMEM] + [VMEM] * (n - 1) + [ANY] * skip,
        out_specs=jax.tree.map(lambda _: VMEM, out_shape),
        compiler_params=pltpu.CompilerParams(vmem_limit_bytes=limit * MIB),
        cost_estimate=pl.CostEstimate(flops=0, bytes_accessed=moved, transcendentals=0),
        name=name,
    )(*ins, *after)


def cores_body(place, basis_hbm, gate_hbm, up_hbm, own, p1, p2, p3, basis, weights, sems):
    depth = basis.shape[0]
    rows = depth // SLICES
    copies = [pltpu.make_async_copy(basis_hbm, basis, sems.at[2 * SLICES])]
    for which, source in enumerate((gate_hbm, up_hbm)):
        for i in range(SLICES):
            at = pl.ds(i * rows, rows)
            sem = sems.at[which * SLICES + i]
            copies.append(pltpu.make_async_copy(source.at[at, :], weights.at[which, at, :], sem))
    for copy in copies:
        copy.start()
    copies[0].wait()
    contract = (((0,), (0,)), ((), ()))
    for which in range(2):
        for copy in copies[1 + which * SLICES : 1 + which * SLICES + SLICES]:
            copy.wait()
        for k, ref in ((2, p2), (1, p1), (3, p3), (0, own)):
            block = lax.rem(place[0] + k, 4)
            part = basis[:, pl.ds(pl.multiple_of(block * 128, 128), 128)]
            total = lax.dot_general(part, weights[which], contract, preferred_element_type=F32)
            ref[which] = total.astype(ref.dtype)


def partial_cores(place, basis, w_gate, w_up):
    depth, width = w_gate.shape
    return pl.pallas_call(
        cores_body,
        out_shape=[like(2, 128, width)] * 4,
        in_specs=[SMEM, HBM, HBM, HBM],
        out_specs=[VMEM] * 4,
        scratch_shapes=[
            pltpu.VMEM(basis.shape, BF16),
            pltpu.VMEM((2, depth, width), BF16),
            pltpu.SemaphoreType.DMA((2 * SLICES + 1,)),
        ],
        compiler_params=pltpu.CompilerParams(vmem_limit_bytes=K1_LIMIT * MIB),
        cost_estimate=pl.CostEstimate(
            flops=4 * depth * basis.shape[1] * width, bytes_accessed=6 * MIB, transcendentals=0
        ),
        name="partial_cores",
    )(place, basis, w_gate, w_up)


def add4(own, r1, r2, r3, at):
    return (own[at].astype(F32) + r1[at].astype(F32)) + (r2[at].astype(F32) + r3[at].astype(F32))


def relay_body(place, own, r1, r2, r3, *outs):
    for k in range(4):
        rows = pl.ds(pl.multiple_of(lax.rem(place[1] + k, 4) * 32, 32), 32)
        first = 0
        for ref in outs[k::4]:
            at = (slice(None), rows, slice(first, first + ref.shape[2]))
            ref[...] = add4(own, r1, r2, r3, at).astype(ref.dtype)
            first += ref.shape[2]


def relay(place, own, pieces, widths, after=()):
    outs = []
    for cols in widths:
        outs += [like(2, 32, cols, kind=F32)] + [like(2, 32, cols)] * 3
    outs = call(relay_body, outs, (place, own, *send(pieces, "a")), after, name="relay")
    return [outs[4 * c : 4 * c + 4] for c in range(len(widths))]


def regroup_body(place, c0, c1, c2, c3, own, r1, r2, r3, *outs):
    first = c0.shape[2]
    for k, (before, ref) in enumerate(zip((c0, c1, c2, c3), outs)):
        rows = pl.ds(pl.multiple_of(lax.rem(place[1] + k, 4) * 32, 32), 32)
        value = add4(own, r1, r2, r3, (slice(None), rows, slice(None)))
        ref[:, :, :first] = before[...]
        ref[:, :, first:] = value.astype(ref.dtype)


def sum4_body(place, own, r1, r2, r3, out):
    out[...] = add4(own, r1, r2, r3, ...).astype(out.dtype)


def add2_body(place, a, b, out):
    out[...] = (a[...].astype(F32) + b[...].astype(F32)).astype(BF16)


def join_body(place, *refs):
    outs = refs[len(refs) // 5 * 4 :]
    for chunk, out in enumerate(outs):
        for k, ref in enumerate(refs[4 * chunk : 4 * chunk + 4]):
            at = pl.ds(pl.multiple_of(lax.rem(place[1] + 4 - k, 4) * 32, 32), 32)
            out[:, at, :] = ref[...]


def main_body(scale, start, place, coeffs, c0, c1, c2, c3, hidden_hbm, *rest):
    first = start == 0
    if first:
        dcoeffs, own, p1, p2, p3, core, grads, terms, hidden, sems = rest
    else:
        before, kept, sent, own, p1, p2, p3, core, grads, terms, hidden, sems = rest
    tiles, tile, cols = hidden.shape
    copies = []
    for i in range(tiles):
        source = hidden_hbm.at[pl.ds(i * tile, tile), pl.ds(start, cols)]
        copies.append(pltpu.make_async_copy(source, hidden.at[i], sems.at[i]))
        copies[i].start()
    for k, ref in enumerate((c0, c1, c2, c3)):
        at = pl.multiple_of(lax.rem(place[0] + 4 - k, 4) * 128, 128)
        core[:, pl.ds(at, 128), :] = ref[...]

    for i in range(tiles):
        rows = slice(i * tile, i * tile + tile)
        x = coeffs[rows, :]
        gate = jnp.dot(x, core[0], preferred_element_type=F32)
        upward = jnp.dot(x, core[1], preferred_element_type=F32)
        sig = 0.5 * jnp.tanh(0.5 * gate) + 0.5
        copies[i].wait()
        scaled = hidden[i].astype(F32) * sig
        terms[0, rows, :] = (scaled * upward * (1.0 + gate * (1.0 - sig))).astype(BF16)
        terms[1, rows, :] = (scaled * gate).astype(BF16)
        contract = (((1,), (1,)), ((), ()))
        total = lax.dot_general(terms[0, rows, :], core[0], contract, preferred_element_type=F32)
        total += lax.dot_general(terms[1, rows, :], core[1], contract, preferred_element_type=F32)
        if first:
            dcoeffs[rows, :] = total
            continue
        total += before[rows, :]
        size = tile // 2
        out_rows = slice(i * size, i * size + size)
        for half in range(2):
            value = total[size * half : size * half + size]

            @pl.when(place[5] == half)
            def _():
                kept[out_rows, :] = value

            @pl.when(place[5] != half)
            def _():
                sent[out_rows, :] = value.astype(BF16)

    contract = (((0,), (0,)), ((), ()))
    for which in range(2):
        grads[which] = lax.dot_general(
            coeffs[...], terms[which], contract, preferred_element_type=F32
        )
    for k, ref in enumerate((own, p1, p2, p3)):
        block = lax.rem(place[0] + k, 4)
        for s in range(8):
            row = block * place[2] + (s // 2) * place[3] + (s % 2) * 64
            for which in range(2):
                value = grads[which, pl.ds(pl.multiple_of(row, 16), 16), :] * scale
                ref[which, s * 16 : s * 16 + 16, :] = value.astype(ref.dtype)


def main(place, coeffs, cores, hidden, before, start, cols, scale):
    tokens, rank = coeffs.shape
    tile = 256
    first = before is None
    if first:
        outs = [like(tokens, rank, kind=F32)]
    else:
        outs = [like(tokens // 2, rank, kind=F32), like(tokens // 2, rank)]
    outs += [like(2, 128, cols, kind=F32)] + [like(2, 128, cols)] * 3
    return pl.pallas_call(
        functools.partial(main_body, scale, start),
        out_shape=outs,
        in_specs=[SMEM] + [VMEM] * 5 + [HBM] + ([] if first else [VMEM]),
        out_specs=[VMEM] * len(outs),
        scratch_shapes=[
            pltpu.VMEM((2, rank, cols), BF16),
            pltpu.VMEM((2, rank, cols), F32),
            pltpu.VMEM((2, tokens, cols), BF16),
            pltpu.VMEM((tokens // tile, tile, cols), BF16),
            pltpu.SemaphoreType.DMA((tokens // tile,)),
        ],
        compiler_params=pltpu.CompilerParams(vmem_limit_bytes=24 * MIB),
        cost_estimate=pl.CostEstimate(
            flops=12 * tokens * rank * cols,
            bytes_accessed=10 * MIB,
            transcendentals=tokens * cols,
        ),
        name="main",
    )(place, coeffs, *cores, hidden, *([] if first else [before]))


def halve_body(place, own, r1, r2, r3, kept, sent):
    for ref, half in ((kept, place[4]), (sent, 1 - place[4])):
        at = (slice(None), pl.ds(pl.multiple_of(half * 16, 16), 16), slice(None))
        ref[...] = add4(own, r1, r2, r3, at).astype(ref.dtype)


def last_body(place, own, other, kept, got, tokens, gate, up):
    tokens[...] = (own[...] + other[...].astype(F32)).astype(BF16)
    gate[...] = kept[0] + got[0].astype(F32)
    up[...] = kept[1] + got[1].astype(F32)


def tokens_body(place, total, got, kept, sent):
    for ref, flip in ((kept, 0), (sent, 1)):
        for i in range(2):
            block = place[6] ^ (flip + 2 * i)
            at = (pl.ds(pl.multiple_of(block * 128, 128), 128), slice(None))
            value = total[at] + got[at].astype(F32)
            ref[128 * i : 128 * i + 128, :] = value.astype(ref.dtype)


def tokens_half_body(place, total, got, kept, sent):
    kept[...] = total[:128] + got[:128].astype(F32)
    sent[...] = (total[128:] + got[128:].astype(F32)).astype(BF16)


def scatter_tokens(place, kept, sent, after):
    rank = kept.shape[1]
    got = lax.ppermute(sent, "tensor", SWAP_CORE)
    for size, body, name in ((256, tokens_body, "tokens"), (128, tokens_half_body, "tokens_half")):
        outs = [like(size, rank, kind=F32), like(size, rank)]
        kept, sent = call(body, outs, (place, kept, got), after, name=name)
        if size == 256:
            got = lax.ppermute(sent, "tensor", SWAP_LOW[0])
    return kept, sent


def local(coeffs, pca_basis, w_gate, w_up, grad_hidden):
    fsdp, tensor = lax.axis_index("fsdp"), lax.axis_index("tensor")
    core, low = tensor & 1, tensor >> 1
    x, z, y = fsdp >> 3, (fsdp >> 2) & 1, fsdp & 3
    a, b = jnp.where(core == 0, y, x), jnp.where(core == 0, x, y)
    stride_a, stride_b = jnp.where(core == 0, 16, 128), jnp.where(core == 0, 128, 16)
    place = jnp.stack([a, b, stride_a, stride_b, z, core, low]).astype(jnp.int32)
    width = w_gate.shape[1]
    scale = 1.0 / math.sqrt(coeffs.shape[0] * 32)
    starts = [sum(WIDTHS[:c]) for c in range(len(WIDTHS))]

    own, *pieces = partial_cores(place, pca_basis, w_gate, w_up)
    halves, cores = [], []
    for cols, (own, *pieces) in zip(WIDTHS, relay(place, own, pieces, WIDTHS)):
        ins = (place, own, *send(pieces, "b"))
        halves.append(call(sum4_body, like(2, 32, cols), ins, name="sum4"))
    for cols, half in zip(WIDTHS, halves):
        ins = (place, half, swap_z(half))
        cores.append(call(add2_body, like(2, 32, cols), ins, halves[-1:], name="add2"))
    ins = [place]
    for core in cores:
        ins += [core] + send([core] * 3, "b")
    blocks = call(join_body, [like(2, 128, cols) for cols in WIDTHS], ins, name="join")
    cores = [[block] + send([block] * 3, "a") for block in blocks]
    total, grads = [None], []
    for start, cols, core in zip(starts, WIDTHS, cores):
        *total, own, p1, p2, p3 = main(
            place, coeffs, core, grad_hidden, total[0], start, cols, scale
        )
        grads.append((own, p1, p2, p3))
    own, *pieces = grads[0]
    parts = list(relay(place, own, pieces, WIDTHS[:1], total[:1])[0])
    kept, sent = total
    sent, _ = lax.optimization_barrier((sent, parts[0]))
    tokens, sent_tokens = scatter_tokens(place, kept, sent, ())
    own, *pieces = grads[1]
    parts += [own] + send(pieces, "a")
    outs = [like(2, 32, width, kind=F32)] + [like(2, 32, width)] * 3
    own, *pieces = call(regroup_body, outs, (place, *parts), (tokens,), name="regroup")
    outs = [like(2, 16, width, kind=F32), like(2, 16, width)]
    kept, sent = call(halve_body, outs, (place, own, *send(pieces, "b")), name="halve")
    ends = [kept, swap_z(sent)]
    sent_tokens, _ = lax.optimization_barrier((sent_tokens, ends[0]))
    other = lax.ppermute(sent_tokens, "tensor", SWAP_LOW[1])
    outs = [like(*tokens.shape)] + [like(16, width, kind=F32)] * 2
    return call(last_body, outs, (place, tokens, other, *ends), name="last")


def solution(mesh):
    placed = (
        P("fsdp", None),
        P("fsdp", None),
        P("fsdp", "tensor"),
        P("fsdp", "tensor"),
        P("fsdp", "tensor"),
    )
    return jax.shard_map(
        local,
        mesh=mesh,
        in_specs=placed,
        out_specs=(P(BOTH, None), P("fsdp", "tensor"), P("fsdp", "tensor")),
        check_vma=False,
    )
```
